128 devices in a mesh: px: 8 (over z, core), py: 16 (over x, y).
Axes of the slice: x: 4, y: 4, z: 4, core: 2. Of those that a mesh axis runs over, the one named last changes fastest.
Arguments:
- sources: bfloat16 [32, 64, 16, 256], P('px', 'py'), may hold values from -6 to 6
- near_codes: int32 [32, 64, 5], P('px', 'py'), may hold values from 0 to 8, as said below
- near_blocks: bfloat16 [32, 64, 5, 256, 256], P('px', 'py'), may hold values from -0.15625 to 0.15625
- basis: float32 [32, 64, 64, 256], P('px', 'py'), may hold values from -0.375 to 0.375
- transfer_one: float32 [32, 64, 64, 64], P('px', 'py'), may hold values from -0.375 to 0.375
- transfer_two: float32 [16, 32, 64, 64], P('px', 'py'), may hold values from -0.375 to 0.375
- transfer_three: float32 [8, 16, 64, 64], P('px', 'py'), may hold values from -0.375 to 0.375
- coupling_zero: float32 [32, 64, 8, 64, 64], P('px', 'py'), may hold values from -0.25 to 0.25
- codes_zero: int32 [32, 64, 8], P('px', 'py'), may hold values from 0 to 24, as said below
- coupling_one: float32 [16, 32, 8, 64, 64], P('px', 'py'), may hold values from -0.5 to 0.5
- codes_one: int32 [16, 32, 8], P('px', 'py'), may hold values from 0 to 24, as said below
- coupling_two: float32 [8, 16, 8, 64, 64], P('px', 'py'), may hold values from -1 to 1
- codes_two: int32 [8, 16, 8], P('px', 'py'), may hold values from 0 to 24, as said below
- coupling_three: float32 [4, 8, 8, 64, 64], replicated, may hold values from -2 to 2
- codes_three: int32 [4, 8, 8], replicated, may hold values from 0 to 24, as said below
Outputs:
- potential: float32 [32, 64, 16, 256], P('px', 'py')
The draws below stay inside these ranges and needn't reach their ends.
Inputs may be any that keep to these rules, and one draw needn't show every extreme that they name: `near_codes`: entry 0 of every list is 4, the block itself; the other entries of a list are distinct codes of other blocks of its 3 x 3 neighbourhood. `codes_zero`: the entries of a list are distinct codes c with max(|c // 5 - 2|, |c % 5 - 2|) = 2. `codes_one`: the entries of a list are distinct codes c with max(|c // 5 - 2|, |c % 5 - 2|) = 2. `codes_two`: the entries of a list are distinct codes c with max(|c // 5 - 2|, |c % 5 - 2|) = 2. `codes_three`: the entries of a list are distinct codes c with max(|c // 5 - 2|, |c % 5 - 2|) = 2.
All inputs are finite; a program needn't handle non-finite values.
Results may differ from the reference program's by a relative error of at most 0.0003.
Values may be sent and summed in bfloat16 or wider, within the bound.
A program may use at most 128 MiB of HBM per device.

```python
import jax
import jax.numpy as jnp
from jax import lax

RHS = 16
LEAF = 256
RANK = 64
NEAR = 5
ILIST = 8
GX = 32
GY = 64


CYCLE_CODES = (0, 1, 2, 3, 4, 5, 9, 10, 14, 15, 19, 20, 21, 22, 23, 24)


OTHER_NEAR = (0, 1, 2, 3, 5, 6, 7, 8)


def pick_codes(key, rows, columns, count, table):
    choices_count = len(table)
    scores = jax.random.randint(key, (rows, columns, choices_count), 0, 1 << 20) * choices_count + jnp.arange(choices_count, dtype=jnp.int32)
    _, chosen = lax.top_k(scores, count)
    return jnp.asarray(table, dtype=jnp.int32)[chosen]


def draw_near_codes(key, part):
    others = pick_codes(jax.random.fold_in(key, 7), GX, GY, NEAR - 1, OTHER_NEAR)
    itself = jnp.full((GX, GY, 1), 4, jnp.int32)
    return jnp.concatenate([itself, others], axis=2)


def draw_codes_zero(key, part):
    return pick_codes(jax.random.fold_in(key, 11), GX, GY, ILIST, CYCLE_CODES)


def draw_codes_one(key, part):
    return pick_codes(jax.random.fold_in(key, 13), GX // 2, GY // 2, ILIST, CYCLE_CODES)


def draw_codes_two(key, part):
    return pick_codes(jax.random.fold_in(key, 17), GX // 4, GY // 4, ILIST, CYCLE_CODES)


def draw_codes_three(key, part):
    return pick_codes(jax.random.fold_in(key, 19), GX // 8, GY // 8, ILIST, CYCLE_CODES)


def level_of(own_key, dims, cuts, smallest, largest):
    def one(axis_at, blocks):
        draws = jax.random.uniform(jax.random.fold_in(jax.random.fold_in(own_key, 6), axis_at), (blocks,), jnp.float32, smallest / len(cuts), largest / len(cuts))
        return jnp.repeat(jnp.exp(draws), dims[axis_at] // blocks).reshape((-1,) + (1,) * (len(dims) - axis_at - 1))

    gain = one(*cuts[0])
    for cut in cuts[1:]:
        gain = gain * one(*cut)
    return gain


def normal_values(key, dims, deviation, reach, split=(), held_as=jnp.bfloat16):
    entries = deviation * jax.random.normal(key, dims, jnp.float32)
    if split:
        entries = entries * level_of(key, dims, split, -0.22, 0.18)
    return jnp.clip(entries, -reach, reach).astype(held_as)


def setup_inputs(seed: int = 0) -> dict:
    seeds = jax.random.split(jax.random.key(seed), 16)
    sources = normal_values(seeds[0], (GX, GY, RHS, LEAF), 1.0, 6.0, ((0, 8), (1, 16)))
    near_codes = draw_near_codes(jax.random.fold_in(seeds[15], 71), 0)
    near_blocks = normal_values(seeds[2], (GX, GY, NEAR, LEAF, LEAF), (LEAF * NEAR) ** -0.5, 0.15625, ((0, 8), (1, 16)))
    basis = normal_values(seeds[3], (GX, GY, RANK, LEAF), LEAF ** -0.5, 0.375, ((0, 8), (1, 16)), jnp.float32)
    transfer_one = normal_values(seeds[4], (GX, GY, RANK, RANK), (4 * RANK) ** -0.5, 0.375, ((0, 8), (1, 16)), jnp.float32)
    transfer_two = normal_values(seeds[5], (GX // 2, GY // 2, RANK, RANK), (4 * RANK) ** -0.5, 0.375, ((0, 8), (1, 16)), jnp.float32)
    transfer_three = normal_values(seeds[6], (GX // 4, GY // 4, RANK, RANK), (4 * RANK) ** -0.5, 0.375, ((0, 8), (1, 16)), jnp.float32)
    coupling_zero = normal_values(seeds[7], (GX, GY, ILIST, RANK, RANK), (RANK * ILIST) ** -0.5, 0.25, ((0, 8), (1, 16)), jnp.float32)
    codes_zero = draw_codes_zero(jax.random.fold_in(seeds[15], 71), 0)
    coupling_one = normal_values(seeds[9], (GX // 2, GY // 2, ILIST, RANK, RANK), (RANK * ILIST // 4) ** -0.5, 0.5, ((0, 8), (1, 16)), jnp.float32)
    codes_one = draw_codes_one(jax.random.fold_in(seeds[15], 71), 0)
    coupling_two = normal_values(seeds[11], (GX // 4, GY // 4, ILIST, RANK, RANK), (RANK * ILIST // 16) ** -0.5, 1.0, ((0, 8), (1, 16)), jnp.float32)
    codes_two = draw_codes_two(jax.random.fold_in(seeds[15], 71), 0)
    coupling_three = normal_values(seeds[13], (GX // 8, GY // 8, ILIST, RANK, RANK), (max(RANK * ILIST // 64, 1)) ** -0.5, 2.0, (), jnp.float32)
    codes_three = draw_codes_three(jax.random.fold_in(seeds[15], 71), 0)
    return dict(sources=sources, near_codes=near_codes, near_blocks=near_blocks, basis=basis, transfer_one=transfer_one, transfer_two=transfer_two, transfer_three=transfer_three, coupling_zero=coupling_zero, codes_zero=codes_zero, coupling_one=coupling_one, codes_one=codes_one, coupling_two=coupling_two, codes_two=codes_two, coupling_three=coupling_three, codes_three=codes_three)


HIGHEST_PRECISION = lax.Precision.HIGHEST
CYCLE_CODES = (0, 1, 2, 3, 4, 5, 9, 10, 14, 15, 19, 20, 21, 22, 23, 24)
NEAR_CODES = (0, 1, 2, 3, 4, 5, 6, 7, 8)


def select_codes(padded, codes, side, candidates):
    rows = codes.shape[0]
    columns = codes.shape[1]
    trailing = padded.shape[2:]
    result = jnp.zeros(codes.shape + trailing, padded.dtype)
    for code in candidates:
        start_row = code // side
        start_column = code % side
        piece = padded[start_row:start_row + rows, start_column:start_column + columns]
        marks = (codes == code).reshape(codes.shape + (1,) * len(trailing))
        result = result + jnp.where(marks, piece[:, :, None], jnp.zeros((), padded.dtype))
    return result


def lift(panel, transfer):
    moved = jnp.einsum("ijrn,ijnm->ijrm", panel, transfer, precision=HIGHEST_PRECISION)
    rows = panel.shape[0] // 2
    columns = panel.shape[1] // 2
    return moved.reshape(rows, 2, columns, 2, moved.shape[2], moved.shape[3]).sum(axis=(1, 3))


def lower(field, transfer):
    spread = jnp.repeat(jnp.repeat(field, 2, axis=0), 2, axis=1)
    return jnp.einsum("ijnm,ijrm->ijrn", transfer, spread, precision=HIGHEST_PRECISION)


def couple_level(panel, coupling, codes):
    padded = jnp.pad(panel, ((2, 2), (2, 2), (0, 0), (0, 0)))
    chosen = select_codes(padded, codes, 5, CYCLE_CODES)
    return jnp.einsum("ijkmn,ijkrn->ijrm", coupling, chosen, precision=HIGHEST_PRECISION)


def reference(sources, near_codes, near_blocks, basis, transfer_one, transfer_two, transfer_three, coupling_zero, codes_zero, coupling_one, codes_one, coupling_two, codes_two, coupling_three, codes_three):
    padded = jnp.pad(sources, ((1, 1), (1, 1), (0, 0), (0, 0)))
    neighbours = select_codes(padded, near_codes, 3, NEAR_CODES)

    def row_product(pair):
        blocks_row, neighbour_row = pair
        return jnp.einsum("jkab,jkrb->jra", blocks_row.astype(jnp.float32), neighbour_row.astype(jnp.float32), precision=HIGHEST_PRECISION)

    near_field = lax.map(row_product, (near_blocks, neighbours))
    panel_zero = jnp.einsum("ijrb,ijmb->ijrm", sources.astype(jnp.float32), basis, precision=HIGHEST_PRECISION)
    panel_one = lift(panel_zero, transfer_one)
    panel_two = lift(panel_one, transfer_two)
    panel_three = lift(panel_two, transfer_three)
    coupled_zero = couple_level(panel_zero, coupling_zero, codes_zero)
    coupled_one = couple_level(panel_one, coupling_one, codes_one)
    coupled_two = couple_level(panel_two, coupling_two, codes_two)
    field_three = couple_level(panel_three, coupling_three, codes_three)
    field_two = coupled_two + lower(field_three, transfer_three)
    field_one = coupled_one + lower(field_two, transfer_two)
    field_zero = coupled_zero + lower(field_one, transfer_one)
    far_field = jnp.einsum("ijmb,ijrm->ijrb", basis, field_zero, precision=HIGHEST_PRECISION)
    return near_field + far_field
```

```python
import jax
import jax.numpy as jnp
from jax import lax
from jax.experimental import pallas as pl
from jax.experimental.pallas import tpu as pltpu
from jax.sharding import PartitionSpec as P

BF16 = jnp.bfloat16
F32 = jnp.float32
MESH = pl.DeviceIdType.MESH

BESIDE = tuple((u, v) for u in (-1, 0, 1) for v in (-1, 0, 1) if (u, v) != (0, 0))
RING = tuple((u, v) for u in range(-2, 3) for v in range(-2, 3) if max(abs(u), abs(v)) == 2)
PAIRS = ((0, 1), (1, 0), (1, 1))


def span(step, count, width, halo):
    if step == 0:
        return pl.ds(width, count)
    if halo:
        return pl.ds(0, width) if step < 0 else pl.ds(width + count, width)
    return pl.ds(width, width) if step < 0 else pl.ds(count, width)


def folded(total):
    return total + pltpu.roll(total, 64, 1)


def halves(value):
    lane = lax.broadcasted_iota(jnp.int32, value.shape, 1)
    high = value.astype(BF16).astype(F32)
    low = value - high
    first = lane < 64
    return jnp.where(first, high, low).astype(BF16), jnp.where(first, low, high).astype(BF16)


def split_rows(matrix):
    high = matrix.astype(BF16)
    low = (matrix - high.astype(F32)).astype(BF16)
    return jnp.concatenate([high, low], axis=0)


def doubled(matrix):
    return split_rows(jnp.concatenate([matrix, matrix], axis=1))


def times(x, w):
    return lax.dot_general(x, w, (((1,), (0,)), ((), ())), preferred_element_type=F32)


def times_t(x, w):
    return lax.dot_general(x, w, (((1,), (1,)), ((), ())), preferred_element_type=F32)


def kernel(
    sources, near_codes, near_blocks, basis, one, two, three, c_zero, k_zero, c_one, k_one,
    c_two, k_two, c_three, k_three, out,
    s_buf, n_buf, b_buf, t1_buf, t2_buf, t3_buf, c0_buf, c1_buf, c2_buf, c3_buf,
    bs_buf, w1_buf, w2_buf, w3_buf, p0, p1, p2, p3, own2, own3, part, swap0, swap1,
    a0_buf, x1_buf, o_buf,
    load_sem, near_sem, zero_sem, out_sem,
    s_send, s_recv, p0_send, p0_recv, p1_send, p1_recv, p2_send, p2_recv, p3_send, p3_recv,
    g_send, g_recv,
):
    px, py = lax.axis_index("px"), lax.axis_index("py")
    nx, ny = lax.axis_size("px"), lax.axis_size("py")
    row3, col3 = lax.div(px, 2), lax.div(py, 2)

    def valid(u, v):
        return (px + u >= 0) & (px + u < nx) & (py + v >= 0) & (py + v < ny)

    loads = [
        pltpu.make_async_copy(sources, s_buf.at[pl.ds(1, 4), pl.ds(1, 4)], load_sem.at[0]),
        pltpu.make_async_copy(basis, b_buf, load_sem.at[1]),
        pltpu.make_async_copy(one, t1_buf, load_sem.at[2]),
        pltpu.make_async_copy(two, t2_buf, load_sem.at[3]),
        pltpu.make_async_copy(three, t3_buf, load_sem.at[4]),
        pltpu.make_async_copy(c_three.at[row3, col3], c3_buf, load_sem.at[5]),
        pltpu.make_async_copy(c_two, c2_buf, load_sem.at[6]),
        pltpu.make_async_copy(c_one, c1_buf, load_sem.at[7]),
    ]

    def near_load(i, j):
        return pltpu.make_async_copy(near_blocks.at[i, j], n_buf.at[i, j], near_sem.at[i, j])

    def zero_load(i):
        return pltpu.make_async_copy(c_zero.at[i], c0_buf.at[i], zero_sem.at[i])

    for load in loads[:5]:
        load.start()
    for i in range(2):
        for j in range(4):
            near_load(i, j).start()
    for load in loads[5:]:
        load.start()
    for i in range(2, 4):
        for j in range(4):
            near_load(i, j).start()
    for i in range(4):
        zero_load(i).start()

    for buf, n, w in ((s_buf, 4, 1), (p0, 4, 2), (p1, 2, 2)):
        for u, v in BESIDE:
            rows, cols = span(u, n, w, True), span(v, n, w, True)
            shape = (rows.size, cols.size) + buf.shape[2:]
            buf[rows, cols] = jnp.zeros(shape, BF16)
    p2[...] = jnp.zeros(p2.shape, BF16)
    p3[...] = jnp.zeros(p3.shape, BF16)

    barrier = pltpu.get_barrier_semaphore()
    partners = BESIDE + RING + tuple((2 * u, 2 * v) for u, v in RING)
    expected = 0
    for u, v in partners:
        ok = valid(u, v)
        expected = expected + ok.astype(jnp.int32)

        @pl.when(ok)
        def _(u=u, v=v):
            pl.semaphore_signal(barrier, inc=1, device_id=(px + u, py + v), device_id_type=MESH)

    def halo_copy(buf, n, w, send, recv, d):
        u, v = BESIDE[d]
        return pltpu.make_async_remote_copy(
            src_ref=buf.at[span(u, n, w, False), span(v, n, w, False)],
            dst_ref=buf.at[span(-u, n, w, True), span(-v, n, w, True)],
            send_sem=send.at[d], recv_sem=recv.at[d],
            device_id=(px + u, py + v), device_id_type=MESH,
        )

    def ring_copy(own, buf, send, recv, d, stride):
        u, v = RING[d]
        return pltpu.make_async_remote_copy(
            src_ref=own, dst_ref=buf.at[2 - u, 2 - v], send_sem=send.at[d], recv_sem=recv.at[d],
            device_id=(px + stride * u, py + stride * v), device_id_type=MESH,
        )

    def pair_copy(d):
        a, b = PAIRS[d]
        x = px + a * (1 - 2 * lax.rem(px, 2))
        y = py + b * (1 - 2 * lax.rem(py, 2))
        return pltpu.make_async_remote_copy(
            src_ref=part.at[0], dst_ref=part.at[d + 1], send_sem=g_send.at[d],
            recv_sem=g_recv.at[d], device_id=(x, y), device_id_type=MESH,
        )

    halos = {
        "s": (s_buf, 4, 1, s_send, s_recv),
        "0": (p0, 4, 2, p0_send, p0_recv),
        "1": (p1, 2, 2, p1_send, p1_recv),
    }
    rings = {"2": (own2, p2, p2_send, p2_recv, 1), "3": (own3, p3, p3_send, p3_recv, 2)}

    def halo_do(name, act, back):
        buf, n, w, send, recv = halos[name]
        for d, (u, v) in enumerate(BESIDE):

            @pl.when(valid(-u, -v) if back else valid(u, v))
            def _(d=d):
                act(halo_copy(buf, n, w, send, recv, d))

    def ring_do(name, act, back):
        own, buf, send, recv, stride = rings[name]
        for d, (u, v) in enumerate(RING):
            u, v = stride * u, stride * v

            @pl.when(valid(-u, -v) if back else valid(u, v))
            def _(d=d):
                act(ring_copy(own, buf, send, recv, d, stride))

    start = lambda copy: copy.start()
    arrived = lambda copy: copy.wait_recv()
    left = lambda copy: copy.wait_send()

    loads[0].wait()
    loads[1].wait()

    def panel_row(i, carry):
        for j in range(4):
            split = split_rows(b_buf[i, j])
            bs_buf[i, j] = split
            value = folded(times_t(s_buf[i + 1, j + 1], split))
            cat, swapped = halves(value)
            p0[i + 2, j + 2] = cat
            swap0[i, j] = swapped
        return carry

    lax.fori_loop(0, 4, panel_row, 0)
    pl.semaphore_wait(barrier, expected)
    halo_do("s", start, False)
    halo_do("0", start, False)

    loads[2].wait()
    loads[3].wait()
    loads[4].wait()
    for i in range(2):
        for j in range(2):
            total = jnp.zeros((32, 128), F32)
            for a in range(2):
                for b in range(2):
                    r, c = 2 * i + a, 2 * j + b
                    w = doubled(t1_buf[r, c])
                    w1_buf[r, c] = w
                    x = jnp.concatenate([p0[r + 2, c + 2], swap0[r, c]], axis=0)
                    total = total + times(x, w)
            cat, swapped = halves(total[:16] + total[16:])
            p1[i + 2, j + 2] = cat
            swap1[i, j] = swapped
    halo_do("1", start, False)
    total = jnp.zeros((32, 128), F32)
    for i in range(2):
        for j in range(2):
            w = doubled(t2_buf[i, j])
            w2_buf[i, j] = w
            x = jnp.concatenate([p1[i + 2, j + 2], swap1[i, j]], axis=0)
            total = total + times(x, w)
    cat, swapped = halves(total[:16] + total[16:])
    own2[...] = cat
    w = doubled(t3_buf[0, 0])
    w3_buf[...] = w
    total = times(jnp.concatenate([cat, swapped], axis=0), w)
    cat, _ = halves(total[:16] + total[16:])
    own3[...] = cat
    ring_do("3", start, False)
    ring_do("2", start, False)

    halo_do("s", arrived, True)

    def near_row(i, carry):
        for j in range(4):
            near_load(i, j).wait()
            total = jnp.zeros((16, 256), F32)
            for k in range(5):
                code = near_codes[i, j, k]
                u = lax.shift_right_logical(code * 11, 5)
                x = s_buf[i + u, j + code - 3 * u]
                total = total + times_t(x, n_buf[i, j, k])
            o_buf[i, j] = total
        return carry

    lax.fori_loop(0, 2, near_row, 0)

    def coupled(matrices, codes, read):
        total = jnp.zeros((16, 128), F32)
        for k in range(8):
            code = codes(k)
            u = lax.shift_right_logical(code * 13, 6)
            total = total + times_t(read(u, code - 5 * u), doubled(matrices(k)))
        return total

    ring_do("3", arrived, True)
    loads[5].wait()
    total = coupled(
        lambda k: c3_buf[k], lambda k: k_three[row3, col3, k], lambda u, v: p3[u, v]
    )
    cat, _ = halves(folded(total))
    part[0] = cat
    for d in range(3):
        pair_copy(d).start()

    lax.fori_loop(2, 4, near_row, 0)

    ring_do("2", arrived, True)
    loads[6].wait()
    field = coupled(lambda k: c2_buf[0, 0, k], lambda k: k_two[0, 0, k], lambda u, v: p2[u, v])
    halo_do("1", arrived, True)
    loads[7].wait()
    ones = []
    for i in range(2):
        for j in range(2):
            ones.append(
                coupled(
                    lambda k: c1_buf[i, j, k],
                    lambda k: k_one[i, j, k],
                    lambda u, v: p1[i + u, j + v],
                )
            )
    halo_do("0", arrived, True)

    def zero_row(i, carry):
        zero_load(i).wait()
        for j in range(4):
            a0_buf[i, j] = coupled(
                lambda k: c0_buf[i, j, k],
                lambda k: k_zero[i, j, k],
                lambda u, v: p0[i + u, j + v],
            )
        return carry

    lax.fori_loop(0, 4, zero_row, 0)

    for d in range(3):
        pair_copy(d).wait_recv()
    w = w3_buf[...]
    for d in range(4):
        field = field + times_t(part[d], w)
    x2, _ = halves(folded(field))
    for i in range(2):
        for j in range(2):
            total = ones[2 * i + j] + times_t(x2, w2_buf[i, j])
            x1_buf[i, j], _ = halves(folded(total))

    def out_copy(i):
        return pltpu.make_async_copy(o_buf.at[i], out.at[i], out_sem.at[i])

    def far_row(i, carry):
        for j in range(4):
            x1 = x1_buf[lax.div(i, 2), j // 2]
            total = a0_buf[i, j] + times_t(x1, w1_buf[i, j])
            cat, swapped = halves(folded(total))
            far = times(jnp.concatenate([cat, swapped], axis=0), bs_buf[i, j])
            o_buf[i, j] = o_buf[i, j] + (far[:16] + far[16:])
        out_copy(i).start()
        return carry

    lax.fori_loop(0, 4, far_row, 0)

    halo_do("s", left, False)
    halo_do("0", left, False)
    halo_do("1", left, False)
    ring_do("2", left, False)
    ring_do("3", left, False)
    for d in range(3):
        pair_copy(d).wait_send()
    for i in range(4):
        out_copy(i).wait()


def on_device(*args):
    smem = {1, 8, 10, 12, 14}
    dma = pltpu.SemaphoreType.DMA
    vmem = pltpu.VMEM
    return pl.pallas_call(
        kernel,
        out_shape=jax.ShapeDtypeStruct((4, 4, 16, 256), F32),
        in_specs=[
            pl.BlockSpec(memory_space=pltpu.SMEM if at in smem else pl.ANY)
            for at in range(len(args))
        ],
        out_specs=pl.BlockSpec(memory_space=pl.ANY),
        scratch_shapes=[
            vmem((6, 6, 16, 256), BF16),
            vmem((4, 4, 5, 256, 256), BF16),
            vmem((4, 4, 64, 256), F32),
            vmem((4, 4, 64, 64), F32),
            vmem((2, 2, 64, 64), F32),
            vmem((1, 1, 64, 64), F32),
            vmem((4, 4, 8, 64, 64), F32),
            vmem((2, 2, 8, 64, 64), F32),
            vmem((1, 1, 8, 64, 64), F32),
            vmem((8, 64, 64), F32),
            vmem((4, 4, 128, 256), BF16),
            vmem((4, 4, 128, 128), BF16),
            vmem((2, 2, 128, 128), BF16),
            vmem((128, 128), BF16),
            vmem((8, 8, 16, 128), BF16),
            vmem((6, 6, 16, 128), BF16),
            vmem((5, 5, 16, 128), BF16),
            vmem((5, 5, 16, 128), BF16),
            vmem((16, 128), BF16),
            vmem((16, 128), BF16),
            vmem((4, 16, 128), BF16),
            vmem((4, 4, 16, 128), BF16),
            vmem((2, 2, 16, 128), BF16),
            vmem((4, 4, 16, 128), F32),
            vmem((2, 2, 16, 128), BF16),
            vmem((4, 4, 16, 256), F32),
            dma((8,)),
            dma((4, 4)),
            dma((4,)),
            dma((4,)),
        ]
        + [dma((8,))] * 6
        + [dma((16,))] * 4
        + [dma((3,))] * 2,
        compiler_params=pltpu.CompilerParams(
            collective_id=0, has_side_effects=True, vmem_limit_bytes=48 * 1024 * 1024
        ),
        name="patches",
    )(*args)


def solution(mesh):
    grid = P("px", "py")
    placed = (grid,) * 13 + (P(), P())
    return jax.shard_map(
        on_device, mesh=mesh, in_specs=placed, out_specs=grid, check_vma=False
    )
```

```python
import jax
import jax.numpy as jnp
from jax import lax
from jax.experimental import pallas as pl
from jax.experimental.pallas import tpu as pltpu
from jax.sharding import PartitionSpec as P

BF16 = jnp.bfloat16
F32 = jnp.float32
MESH = pl.DeviceIdType.MESH

BESIDE = tuple((u, v) for u in (-1, 0, 1) for v in (-1, 0, 1) if (u, v) != (0, 0))
RING = tuple((u, v) for u in range(-2, 3) for v in range(-2, 3) if max(abs(u), abs(v)) == 2)
PAIRS = ((0, 1), (1, 0), (1, 1))


def span(step, count, width, halo):
    if step == 0:
        return pl.ds(width, count)
    if halo:
        return pl.ds(0, width) if step < 0 else pl.ds(width + count, width)
    return pl.ds(width, width) if step < 0 else pl.ds(count, width)


def folded(total):
    return total + pltpu.roll(total, 64, 1)


def halves(value):
    lane = lax.broadcasted_iota(jnp.int32, value.shape, 1)
    high = value.astype(BF16).astype(F32)
    low = value - high
    first = lane < 64
    return jnp.where(first, high, low).astype(BF16), jnp.where(first, low, high).astype(BF16)


def split_rows(matrix):
    high = matrix.astype(BF16)
    low = (matrix - high.astype(F32)).astype(BF16)
    return jnp.concatenate([high, low], axis=0)


def doubled(matrix):
    return split_rows(jnp.concatenate([matrix, matrix], axis=1))


def times(x, w):
    return lax.dot_general(x, w, (((1,), (0,)), ((), ())), preferred_element_type=F32)


def times_t(x, w):
    return lax.dot_general(x, w, (((1,), (1,)), ((), ())), preferred_element_type=F32)


def kernel(
    sources, h_near, near_blocks, basis, one, two, three, c_zero, h_zero, c_one, h_one,
    c_two, h_two, c_three, h_three, o_buf,
    near_codes, k_zero, k_one, k_two, k_three,
    s_buf, n_buf, b_buf, t1_buf, t2_buf, t3_buf, c0_buf, c1_buf, c2_buf, c3_buf,
    bs_buf, w1_buf, w2_buf, w3_buf, p0, p1, p2, p3, own2, own3, part, swap0, swap1,
    a0_buf, x1_buf,
    load_sem, near_sem, zero_sem, code_sem,
    s_send, s_recv, p0_send, p0_recv, p1_send, p1_recv, p2_send, p2_recv, p3_send, p3_recv,
    g_send, g_recv,
):
    px, py = lax.axis_index("px"), lax.axis_index("py")
    nx, ny = lax.axis_size("px"), lax.axis_size("py")
    row3, col3 = lax.div(px, 2), lax.div(py, 2)

    def valid(u, v):
        return (px + u >= 0) & (px + u < nx) & (py + v >= 0) & (py + v < ny)

    loads = [
        pltpu.make_async_copy(sources, s_buf.at[pl.ds(1, 4), pl.ds(1, 4)], load_sem.at[0]),
        pltpu.make_async_copy(basis, b_buf, load_sem.at[1]),
        pltpu.make_async_copy(one, t1_buf, load_sem.at[2]),
        pltpu.make_async_copy(two, t2_buf, load_sem.at[3]),
        pltpu.make_async_copy(three, t3_buf, load_sem.at[4]),
        pltpu.make_async_copy(c_three.at[row3, col3], c3_buf, load_sem.at[5]),
        pltpu.make_async_copy(c_two, c2_buf, load_sem.at[6]),
        pltpu.make_async_copy(c_one, c1_buf, load_sem.at[7]),
    ]

    def near_load(i, j):
        return pltpu.make_async_copy(near_blocks.at[i, j], n_buf.at[i, j], near_sem.at[i, j])

    def zero_load(i):
        return pltpu.make_async_copy(c_zero.at[i], c0_buf.at[i], zero_sem.at[i])

    codes = [
        pltpu.make_async_copy(h_near, near_codes, code_sem.at[0]),
        pltpu.make_async_copy(h_zero, k_zero, code_sem.at[1]),
        pltpu.make_async_copy(h_one, k_one, code_sem.at[2]),
        pltpu.make_async_copy(h_two, k_two, code_sem.at[3]),
        pltpu.make_async_copy(h_three, k_three, code_sem.at[4]),
    ]
    for load in loads[:5] + codes:
        load.start()
    for i in range(2):
        for j in range(4):
            near_load(i, j).start()
    for load in loads[5:]:
        load.start()
    for i in range(2, 4):
        for j in range(4):
            near_load(i, j).start()
    for i in range(4):
        zero_load(i).start()

    for buf, n, w in ((s_buf, 4, 1), (p0, 4, 2), (p1, 2, 2)):
        for u, v in BESIDE:
            rows, cols = span(u, n, w, True), span(v, n, w, True)
            shape = (rows.size, cols.size) + buf.shape[2:]
            buf[rows, cols] = jnp.zeros(shape, BF16)
    p2[...] = jnp.zeros(p2.shape, BF16)
    p3[...] = jnp.zeros(p3.shape, BF16)

    barrier = pltpu.get_barrier_semaphore()
    partners = BESIDE + RING + tuple((2 * u, 2 * v) for u, v in RING)
    expected = 0
    for u, v in partners:
        ok = valid(u, v)
        expected = expected + ok.astype(jnp.int32)

        @pl.when(ok)
        def _(u=u, v=v):
            pl.semaphore_signal(barrier, inc=1, device_id=(px + u, py + v), device_id_type=MESH)

    def halo_copy(buf, n, w, send, recv, d):
        u, v = BESIDE[d]
        return pltpu.make_async_remote_copy(
            src_ref=buf.at[span(u, n, w, False), span(v, n, w, False)],
            dst_ref=buf.at[span(-u, n, w, True), span(-v, n, w, True)],
            send_sem=send.at[d], recv_sem=recv.at[d],
            device_id=(px + u, py + v), device_id_type=MESH,
        )

    def ring_copy(own, buf, send, recv, d, stride):
        u, v = RING[d]
        return pltpu.make_async_remote_copy(
            src_ref=own, dst_ref=buf.at[2 - u, 2 - v], send_sem=send.at[d], recv_sem=recv.at[d],
            device_id=(px + stride * u, py + stride * v), device_id_type=MESH,
        )

    def pair_copy(d):
        a, b = PAIRS[d]
        x = px + a * (1 - 2 * lax.rem(px, 2))
        y = py + b * (1 - 2 * lax.rem(py, 2))
        return pltpu.make_async_remote_copy(
            src_ref=part.at[0], dst_ref=part.at[d + 1], send_sem=g_send.at[d],
            recv_sem=g_recv.at[d], device_id=(x, y), device_id_type=MESH,
        )

    halos = {
        "s": (s_buf, 4, 1, s_send, s_recv),
        "0": (p0, 4, 2, p0_send, p0_recv),
        "1": (p1, 2, 2, p1_send, p1_recv),
    }
    rings = {"2": (own2, p2, p2_send, p2_recv, 1), "3": (own3, p3, p3_send, p3_recv, 2)}

    def halo_do(name, act, back):
        buf, n, w, send, recv = halos[name]
        for d, (u, v) in enumerate(BESIDE):

            @pl.when(valid(-u, -v) if back else valid(u, v))
            def _(d=d):
                act(halo_copy(buf, n, w, send, recv, d))

    def ring_do(name, act, back):
        own, buf, send, recv, stride = rings[name]
        for d, (u, v) in enumerate(RING):
            u, v = stride * u, stride * v

            @pl.when(valid(-u, -v) if back else valid(u, v))
            def _(d=d):
                act(ring_copy(own, buf, send, recv, d, stride))

    start = lambda copy: copy.start()
    arrived = lambda copy: copy.wait_recv()
    left = lambda copy: copy.wait_send()

    loads[0].wait()
    loads[1].wait()

    def panel_row(i, carry):
        for j in range(4):
            split = split_rows(b_buf[i, j])
            bs_buf[i, j] = split
            value = folded(times_t(s_buf[i + 1, j + 1], split))
            cat, swapped = halves(value)
            p0[i + 2, j + 2] = cat
            swap0[i, j] = swapped
        return carry

    lax.fori_loop(0, 4, panel_row, 0)
    pl.semaphore_wait(barrier, expected)
    halo_do("s", start, False)
    halo_do("0", start, False)

    loads[2].wait()
    loads[3].wait()
    loads[4].wait()
    for i in range(2):
        for j in range(2):
            total = jnp.zeros((32, 128), F32)
            for a in range(2):
                for b in range(2):
                    r, c = 2 * i + a, 2 * j + b
                    w = doubled(t1_buf[r, c])
                    w1_buf[r, c] = w
                    x = jnp.concatenate([p0[r + 2, c + 2], swap0[r, c]], axis=0)
                    total = total + times(x, w)
            cat, swapped = halves(total[:16] + total[16:])
            p1[i + 2, j + 2] = cat
            swap1[i, j] = swapped
    halo_do("1", start, False)
    total = jnp.zeros((32, 128), F32)
    for i in range(2):
        for j in range(2):
            w = doubled(t2_buf[i, j])
            w2_buf[i, j] = w
            x = jnp.concatenate([p1[i + 2, j + 2], swap1[i, j]], axis=0)
            total = total + times(x, w)
    cat, swapped = halves(total[:16] + total[16:])
    own2[...] = cat
    w = doubled(t3_buf[0, 0])
    w3_buf[...] = w
    total = times(jnp.concatenate([cat, swapped], axis=0), w)
    cat, _ = halves(total[:16] + total[16:])
    own3[...] = cat
    ring_do("3", start, False)
    ring_do("2", start, False)

    for load in codes:
        load.wait()
    halo_do("s", arrived, True)

    def near_row(i, carry):
        for j in range(4):
            near_load(i, j).wait()
            total = jnp.zeros((16, 256), F32)
            for k in range(5):
                code = near_codes[i, j, k]
                u = lax.shift_right_logical(code * 11, 5)
                x = s_buf[i + u, j + code - 3 * u]
                total = total + times_t(x, n_buf[i, j, k])
            o_buf[i, j] = total
        return carry

    lax.fori_loop(0, 2, near_row, 0)

    def coupled(matrices, codes, read):
        total = jnp.zeros((16, 128), F32)
        for k in range(8):
            code = codes(k)
            u = lax.shift_right_logical(code * 13, 6)
            total = total + times_t(read(u, code - 5 * u), doubled(matrices(k)))
        return total

    ring_do("3", arrived, True)
    loads[5].wait()
    total = coupled(
        lambda k: c3_buf[k], lambda k: k_three[row3, col3, k], lambda u, v: p3[u, v]
    )
    cat, _ = halves(folded(total))
    part[0] = cat
    for d in range(3):
        pair_copy(d).start()

    lax.fori_loop(2, 4, near_row, 0)

    ring_do("2", arrived, True)
    loads[6].wait()
    field = coupled(lambda k: c2_buf[0, 0, k], lambda k: k_two[0, 0, k], lambda u, v: p2[u, v])
    halo_do("1", arrived, True)
    loads[7].wait()
    ones = []
    for i in range(2):
        for j in range(2):
            ones.append(
                coupled(
                    lambda k: c1_buf[i, j, k],
                    lambda k: k_one[i, j, k],
                    lambda u, v: p1[i + u, j + v],
                )
            )
    halo_do("0", arrived, True)

    def zero_row(i, carry):
        zero_load(i).wait()
        for j in range(4):
            a0_buf[i, j] = coupled(
                lambda k: c0_buf[i, j, k],
                lambda k: k_zero[i, j, k],
                lambda u, v: p0[i + u, j + v],
            )
        return carry

    lax.fori_loop(0, 4, zero_row, 0)

    for d in range(3):
        pair_copy(d).wait_recv()
    w = w3_buf[...]
    for d in range(4):
        field = field + times_t(part[d], w)
    x2, _ = halves(folded(field))
    for i in range(2):
        for j in range(2):
            total = ones[2 * i + j] + times_t(x2, w2_buf[i, j])
            x1_buf[i, j], _ = halves(folded(total))

    def far_row(i, carry):
        for j in range(4):
            x1 = x1_buf[lax.div(i, 2), j // 2]
            total = a0_buf[i, j] + times_t(x1, w1_buf[i, j])
            cat, swapped = halves(folded(total))
            far = times(jnp.concatenate([cat, swapped], axis=0), bs_buf[i, j])
            o_buf[i, j] = o_buf[i, j] + (far[:16] + far[16:])
        return carry

    lax.fori_loop(0, 4, far_row, 0)

    halo_do("s", left, False)
    halo_do("0", left, False)
    halo_do("1", left, False)
    ring_do("2", left, False)
    ring_do("3", left, False)
    for d in range(3):
        pair_copy(d).wait_send()


def on_device(*args):
    dma = pltpu.SemaphoreType.DMA
    vmem = pltpu.VMEM
    return pl.pallas_call(
        kernel,
        out_shape=jax.ShapeDtypeStruct((4, 4, 16, 256), F32),
        in_specs=[pl.BlockSpec(memory_space=pltpu.HBM)] * len(args),
        out_specs=pl.BlockSpec(memory_space=pltpu.VMEM),
        scratch_shapes=[
            pltpu.SMEM((4, 4, 5), jnp.int32),
            pltpu.SMEM((4, 4, 8), jnp.int32),
            pltpu.SMEM((2, 2, 8), jnp.int32),
            pltpu.SMEM((1, 1, 8), jnp.int32),
            pltpu.SMEM(args[14].shape, jnp.int32),
            vmem((6, 6, 16, 256), BF16),
            vmem((4, 4, 5, 256, 256), BF16),
            vmem((4, 4, 64, 256), F32),
            vmem((4, 4, 64, 64), F32),
            vmem((2, 2, 64, 64), F32),
            vmem((1, 1, 64, 64), F32),
            vmem((4, 4, 8, 64, 64), F32),
            vmem((2, 2, 8, 64, 64), F32),
            vmem((1, 1, 8, 64, 64), F32),
            vmem((8, 64, 64), F32),
            vmem((4, 4, 128, 256), BF16),
            vmem((4, 4, 128, 128), BF16),
            vmem((2, 2, 128, 128), BF16),
            vmem((128, 128), BF16),
            vmem((8, 8, 16, 128), BF16),
            vmem((6, 6, 16, 128), BF16),
            vmem((5, 5, 16, 128), BF16),
            vmem((5, 5, 16, 128), BF16),
            vmem((16, 128), BF16),
            vmem((16, 128), BF16),
            vmem((4, 16, 128), BF16),
            vmem((4, 4, 16, 128), BF16),
            vmem((2, 2, 16, 128), BF16),
            vmem((4, 4, 16, 128), F32),
            vmem((2, 2, 16, 128), BF16),
            dma((8,)),
            dma((4, 4)),
            dma((4,)),
            dma((5,)),
        ]
        + [dma((8,))] * 6
        + [dma((16,))] * 4
        + [dma((3,))] * 2,
        compiler_params=pltpu.CompilerParams(
            collective_id=0, has_side_effects=True, vmem_limit_bytes=60 * 1024 * 1024
        ),
        name="patches",
    )(*args)


def solution(mesh):
    grid = P("px", "py")
    placed = (grid,) * 13 + (P(), P())
    return jax.shard_map(
        on_device, mesh=mesh, in_specs=placed, out_specs=grid, check_vma=False
    )
```

```python
import jax
import jax.numpy as jnp
from jax import lax
from jax.experimental import pallas as pl
from jax.experimental.pallas import tpu as pltpu
from jax.sharding import PartitionSpec as P

BF16 = jnp.bfloat16
F32 = jnp.float32
MESH = pl.DeviceIdType.MESH

BESIDE = tuple((u, v) for u in (-1, 0, 1) for v in (-1, 0, 1) if (u, v) != (0, 0))
RING = tuple((u, v) for u in range(-2, 3) for v in range(-2, 3) if max(abs(u), abs(v)) == 2)
PAIRS = ((0, 1), (1, 0), (1, 1))


def span(step, count, width, halo):
    if step == 0:
        return pl.ds(width, count)
    if halo:
        return pl.ds(0, width) if step < 0 else pl.ds(width + count, width)
    return pl.ds(width, width) if step < 0 else pl.ds(count, width)


def edge_of(step, count, width):
    if step == 0:
        return pl.ds(0, count)
    return pl.ds(0, width) if step < 0 else pl.ds(count - width, width)


def folded(total):
    return total + pltpu.roll(total, 64, 1)


def halves(value):
    lane = lax.broadcasted_iota(jnp.int32, value.shape, 1)
    high = value.astype(BF16).astype(F32)
    low = value - high
    first = lane < 64
    return jnp.where(first, high, low).astype(BF16), jnp.where(first, low, high).astype(BF16)


def split_rows(matrix):
    high = matrix.astype(BF16)
    low = (matrix - high.astype(F32)).astype(BF16)
    return jnp.concatenate([high, low], axis=0)


def doubled(matrix):
    return split_rows(jnp.concatenate([matrix, matrix], axis=1))


def times(x, w):
    return lax.dot_general(x, w, (((1,), (0,)), ((), ())), preferred_element_type=F32)


def times_t(x, w):
    return lax.dot_general(x, w, (((1,), (1,)), ((), ())), preferred_element_type=F32)


def kernel(
    sources, h_near, near_blocks, basis, one, two, three, c_zero, h_zero, c_one, h_one,
    c_two, h_two, c_three, h_three, out,
    near_codes, k_zero, k_one, k_two, k_three,
    s_own, s_buf, n_buf, b_buf, t1_buf, t2_buf, t3_buf, c0_buf, c1_buf, c2_buf, c3_buf,
    bs_buf, w1_buf, p0, p1, p2, p3, own2, own3, part, o_buf,
    load_sem, near_sem, zero_sem, code_sem, out_sem,
    s_send, s_recv, p0_send, p0_recv, p1_send, p1_recv, p2_send, p2_recv, p3_send, p3_recv,
    g_send, g_recv,
):
    px, py = lax.axis_index("px"), lax.axis_index("py")
    nx, ny = lax.axis_size("px"), lax.axis_size("py")
    row3, col3 = lax.div(px, 2), lax.div(py, 2)
    blocks = tuple((i, j) for i in range(4) for j in range(4))
    inner = tuple((i, j) for i in (1, 2) for j in (1, 2))
    edge = tuple(block for block in blocks if block not in inner)

    def valid(u, v):
        ok = None
        for at, step, count in ((px, u, nx), (py, v, ny)):
            if step:
                here = at + step < count if step > 0 else at + step >= 0
                ok = here if ok is None else ok & here
        return ok

    loads = [
        pltpu.make_async_copy(sources, s_own, load_sem.at[0]),
        pltpu.make_async_copy(basis, b_buf, load_sem.at[1]),
        pltpu.make_async_copy(one, t1_buf, load_sem.at[2]),
        pltpu.make_async_copy(two, t2_buf, load_sem.at[3]),
        pltpu.make_async_copy(three, t3_buf, load_sem.at[4]),
        pltpu.make_async_copy(c_three.at[row3, col3], c3_buf, load_sem.at[5]),
        pltpu.make_async_copy(c_two, c2_buf, load_sem.at[6]),
        pltpu.make_async_copy(c_one, c1_buf, load_sem.at[7]),
        pltpu.make_async_copy(sources, s_buf.at[pl.ds(1, 4), pl.ds(1, 4)], load_sem.at[8]),
    ]
    pieces = (
        (pl.ds(0, 4), pl.ds(0, 4), pl.ds(0, 1)),
        (pl.ds(1, 2), pl.ds(1, 2), pl.ds(1, 4)),
        (pl.ds(0, 1), pl.ds(0, 4), pl.ds(1, 4)),
        (pl.ds(1, 2), pl.ds(0, 1), pl.ds(1, 4)),
        (pl.ds(1, 2), pl.ds(3, 1), pl.ds(1, 4)),
        (pl.ds(3, 1), pl.ds(0, 4), pl.ds(1, 4)),
    )
    near_loads = [
        pltpu.make_async_copy(near_blocks.at[piece], n_buf.at[piece], near_sem.at[at])
        for at, piece in enumerate(pieces)
    ]
    zero_loads = [
        pltpu.make_async_copy(c_zero.at[i], c0_buf.at[i], zero_sem.at[i]) for i in range(4)
    ]
    codes = [
        pltpu.make_async_copy(h_near, near_codes, code_sem.at[0]),
        pltpu.make_async_copy(h_zero, k_zero, code_sem.at[1]),
        pltpu.make_async_copy(h_one, k_one, code_sem.at[2]),
        pltpu.make_async_copy(h_two, k_two, code_sem.at[3]),
        pltpu.make_async_copy(h_three, k_three, code_sem.at[4]),
    ]
    for load in loads[:5] + codes:
        load.start()

    for buf, n, w in ((s_buf, 4, 1), (p0, 4, 2), (p1, 2, 2)):
        for u, v in BESIDE:
            rows, cols = span(u, n, w, True), span(v, n, w, True)
            shape = (rows.size, cols.size) + buf.shape[2:]
            buf[rows, cols] = jnp.zeros(shape, BF16)
    p2[...] = jnp.zeros(p2.shape, BF16)
    p3[...] = jnp.zeros(p3.shape, BF16)

    barrier = pltpu.get_barrier_semaphore()
    partners = BESIDE + RING + tuple((2 * u, 2 * v) for u, v in RING)
    expected = 0
    for u, v in partners:
        ok = valid(u, v)
        expected = expected + ok.astype(jnp.int32)

        @pl.when(ok)
        def _(u=u, v=v):
            pl.semaphore_signal(barrier, inc=1, device_id=(px + u, py + v), device_id_type=MESH)

    for load in near_loads + loads[5:] + zero_loads:
        load.start()

    def halo_copy(buf, n, w, send, recv, d, own=None):
        u, v = BESIDE[d]
        if own is None:
            src = buf.at[span(u, n, w, False), span(v, n, w, False)]
        else:
            src = own.at[edge_of(u, n, w), edge_of(v, n, w)]
        return pltpu.make_async_remote_copy(
            src_ref=src,
            dst_ref=buf.at[span(-u, n, w, True), span(-v, n, w, True)],
            send_sem=send.at[d], recv_sem=recv.at[d],
            device_id=(px + u, py + v), device_id_type=MESH,
        )

    def ring_copy(own, buf, send, recv, d, stride):
        u, v = RING[d]
        return pltpu.make_async_remote_copy(
            src_ref=own, dst_ref=buf.at[2 - u, 2 - v], send_sem=send.at[d], recv_sem=recv.at[d],
            device_id=(px + stride * u, py + stride * v), device_id_type=MESH,
        )

    def pair_copy(d):
        a, b = PAIRS[d]
        x = px + a * (1 - 2 * lax.rem(px, 2))
        y = py + b * (1 - 2 * lax.rem(py, 2))
        return pltpu.make_async_remote_copy(
            src_ref=part.at[0], dst_ref=part.at[d + 1], send_sem=g_send.at[d],
            recv_sem=g_recv.at[d], device_id=(x, y), device_id_type=MESH,
        )

    halos = {
        "s": (s_buf, 4, 1, s_send, s_recv),
        "0": (p0, 4, 2, p0_send, p0_recv),
        "1": (p1, 2, 2, p1_send, p1_recv),
    }
    rings = {"2": (own2, p2, p2_send, p2_recv, 1), "3": (own3, p3, p3_send, p3_recv, 2)}

    def halo_do(name, act, back):
        buf, n, w, send, recv = halos[name]
        for d, (u, v) in enumerate(BESIDE):

            @pl.when(valid(-u, -v) if back else valid(u, v))
            def _(d=d):
                act(halo_copy(buf, n, w, send, recv, d, s_own if name == "s" else None))

    def ring_do(name, act, back):
        own, buf, send, recv, stride = rings[name]
        for d, (u, v) in enumerate(RING):
            u, v = stride * u, stride * v

            @pl.when(valid(-u, -v) if back else valid(u, v))
            def _(d=d):
                act(ring_copy(own, buf, send, recv, d, stride))

    start = lambda copy: copy.start()
    arrived = lambda copy: copy.wait_recv()
    left = lambda copy: copy.wait_send()

    for load in loads[:5]:
        load.wait()
    totals = {}
    for i, j in blocks:
        split = split_rows(b_buf[i, j])
        bs_buf[i, j] = split
        totals[i, j] = times_t(s_own[i, j], split)
    below = {}
    for i, j in blocks:
        below[i, j] = halves(folded(totals[i, j]))
        p0[i + 2, j + 2] = below[i, j][0]
    above = {}
    for i in range(2):
        for j in range(2):
            total = jnp.zeros((32, 128), F32)
            for a in range(2):
                for b in range(2):
                    r, c = 2 * i + a, 2 * j + b
                    w = doubled(t1_buf[r, c])
                    w1_buf[r, c] = w
                    total = total + times(jnp.concatenate(below[r, c], axis=0), w)
            above[i, j] = halves(total[:16] + total[16:])
            p1[i + 2, j + 2] = above[i, j][0]
    total = jnp.zeros((32, 128), F32)
    for i in range(2):
        for j in range(2):
            total = total + times(jnp.concatenate(above[i, j], axis=0), doubled(t2_buf[i, j]))
    pair = halves(total[:16] + total[16:])
    own2[...] = pair[0]
    total = times(jnp.concatenate(pair, axis=0), doubled(t3_buf[0, 0]))
    own3[...] = halves(total[:16] + total[16:])[0]

    pl.semaphore_wait(barrier, expected)
    halo_do("s", start, False)
    ring_do("3", start, False)
    ring_do("2", start, False)
    halo_do("1", start, False)
    halo_do("0", start, False)

    def near_product(i, j, k, buf, shift):
        code = near_codes[i, j, k]
        u = lax.shift_right_logical(code * 11, 5)
        x = buf[i + u - shift, j + code - 3 * u - shift]
        return times_t(x, n_buf[i, j, k])

    for load in codes:
        load.wait()
    near_loads[0].wait()
    near_loads[1].wait()
    for i, j in blocks:
        total = times_t(s_own[i, j], n_buf[i, j, 0])
        if (i, j) in inner:
            for k in range(1, 5):
                total = total + near_product(i, j, k, s_own, 1)
        o_buf[i, j] = total

    loads[8].wait()
    halo_do("s", arrived, True)

    def near_edge(some):
        for i, j in some:
            total = o_buf[i, j]
            for k in range(1, 5):
                total = total + near_product(i, j, k, s_buf, 0)
            o_buf[i, j] = total

    def coupled(matrices, codes, read, total=None):
        for k in range(0, 8, 2):
            xs, ws = [], []
            for q in (k, k + 1):
                code = codes(q)
                u = lax.shift_right_logical(code * 13, 6)
                xs.append(read(u, code - 5 * u))
                ws.append(doubled(matrices(q)))
            term = times_t(jnp.concatenate(xs, axis=1), jnp.concatenate(ws, axis=1))
            total = term if total is None else total + term
        return total

    ring_do("3", arrived, True)
    loads[5].wait()
    for load in near_loads[2:4]:
        load.wait()
    total = coupled(
        lambda k: c3_buf[k], lambda k: k_three[row3, col3, k], lambda u, v: p3[u, v]
    )
    part[0] = halves(folded(total))[0]
    near_edge(edge[:4] + ((1, 0), (2, 0)))
    for d in range(3):
        pair_copy(d).start()
    for load in near_loads[4:]:
        load.wait()
    near_edge(((1, 3), (2, 3)) + edge[8:])

    ring_do("2", arrived, True)
    halo_do("1", arrived, True)
    halo_do("0", arrived, True)
    for load in loads[6:8] + zero_loads:
        load.wait()
    field = coupled(lambda k: c2_buf[0, 0, k], lambda k: k_two[0, 0, k], lambda u, v: p2[u, v])
    ones = {}
    for i in range(2):
        for j in range(2):
            ones[i, j] = coupled(
                lambda k: c1_buf[i, j, k],
                lambda k: k_one[i, j, k],
                lambda u, v: p1[i + u, j + v],
            )
    zeros = {}
    for i, j in blocks:
        zeros[i, j] = coupled(
            lambda k: c0_buf[i, j, k],
            lambda k: k_zero[i, j, k],
            lambda u, v: p0[i + u, j + v],
        )

    for d in range(3):
        pair_copy(d).wait_recv()
    w = doubled(t3_buf[0, 0])
    for d in range(4):
        field = field + times_t(part[d], w)
    x2 = halves(folded(field))[0]
    x1 = {}
    for i in range(2):
        for j in range(2):
            total = ones[i, j] + times_t(x2, doubled(t2_buf[i, j]))
            x1[i, j] = halves(folded(total))[0]
    for i, j in blocks:
        zeros[i, j] = zeros[i, j] + times_t(x1[i // 2, j // 2], w1_buf[i, j])
    outs = [pltpu.make_async_copy(o_buf.at[i], out.at[i], out_sem.at[i]) for i in range(4)]
    for i, j in blocks:
        pair = halves(folded(zeros[i, j]))
        far = times(jnp.concatenate(pair, axis=0), bs_buf[i, j])
        o_buf[i, j] = o_buf[i, j] + (far[:16] + far[16:])
        if j == 3:
            outs[i].start()

    halo_do("s", left, False)
    halo_do("0", left, False)
    halo_do("1", left, False)
    ring_do("2", left, False)
    ring_do("3", left, False)
    for d in range(3):
        pair_copy(d).wait_send()
    for copy in outs:
        copy.wait()


def on_device(*args):
    dma = pltpu.SemaphoreType.DMA
    vmem = pltpu.VMEM
    return pl.pallas_call(
        kernel,
        out_shape=jax.ShapeDtypeStruct((4, 4, 16, 256), F32),
        in_specs=[pl.BlockSpec(memory_space=pltpu.HBM)] * len(args),
        out_specs=pl.BlockSpec(memory_space=pltpu.HBM),
        scratch_shapes=[
            pltpu.SMEM((4, 4, 5), jnp.int32),
            pltpu.SMEM((4, 4, 8), jnp.int32),
            pltpu.SMEM((2, 2, 8), jnp.int32),
            pltpu.SMEM((1, 1, 8), jnp.int32),
            pltpu.SMEM(args[14].shape, jnp.int32),
            vmem((4, 4, 16, 256), BF16),
            vmem((6, 6, 16, 256), BF16),
            vmem((4, 4, 5, 256, 256), BF16),
            vmem((4, 4, 64, 256), F32),
            vmem((4, 4, 64, 64), F32),
            vmem((2, 2, 64, 64), F32),
            vmem((1, 1, 64, 64), F32),
            vmem((4, 4, 8, 64, 64), F32),
            vmem((2, 2, 8, 64, 64), F32),
            vmem((1, 1, 8, 64, 64), F32),
            vmem((8, 64, 64), F32),
            vmem((4, 4, 128, 256), BF16),
            vmem((4, 4, 128, 128), BF16),
            vmem((8, 8, 16, 128), BF16),
            vmem((6, 6, 16, 128), BF16),
            vmem((5, 5, 16, 128), BF16),
            vmem((5, 5, 16, 128), BF16),
            vmem((16, 128), BF16),
            vmem((16, 128), BF16),
            vmem((4, 16, 128), BF16),
            vmem((4, 4, 16, 256), F32),
            dma((9,)),
            dma((6,)),
            dma((4,)),
            dma((5,)),
            dma((4,)),
        ]
        + [dma((8,))] * 6
        + [dma((16,))] * 4
        + [dma((3,))] * 2,
        compiler_params=pltpu.CompilerParams(
            collective_id=0, has_side_effects=True, vmem_limit_bytes=60 * 1024 * 1024
        ),
        name="patches",
    )(*args)


def solution(mesh):
    grid = P("px", "py")
    placed = (grid,) * 13 + (P(), P())
    return jax.shard_map(
        on_device, mesh=mesh, in_specs=placed, out_specs=grid, check_vma=False
    )
```

```python
import jax
import jax.numpy as jnp
from jax import lax
from jax.experimental import pallas as pl
from jax.experimental.pallas import tpu as pltpu
from jax.sharding import PartitionSpec as P

BF16 = jnp.bfloat16
F32 = jnp.float32
MESH = pl.DeviceIdType.MESH

BESIDE = tuple((u, v) for u in (-1, 0, 1) for v in (-1, 0, 1) if (u, v) != (0, 0))
RING = tuple((u, v) for u in range(-2, 3) for v in range(-2, 3) if max(abs(u), abs(v)) == 2)
PAIRS = ((0, 1), (1, 0), (1, 1))


def span(step, count, width, halo):
    if step == 0:
        return pl.ds(width, count)
    if halo:
        return pl.ds(0, width) if step < 0 else pl.ds(width + count, width)
    return pl.ds(width, width) if step < 0 else pl.ds(count, width)


def edge_of(step, count, width):
    if step == 0:
        return pl.ds(0, count)
    return pl.ds(0, width) if step < 0 else pl.ds(count - width, width)


def folded(total):
    return total + pltpu.roll(total, 64, 1)


def halves(value):
    lane = lax.broadcasted_iota(jnp.int32, value.shape, 1)
    high = value.astype(BF16).astype(F32)
    low = value - high
    first = lane < 64
    return jnp.where(first, high, low).astype(BF16), jnp.where(first, low, high).astype(BF16)


def split_rows(matrix):
    high = matrix.astype(BF16)
    low = (matrix - high.astype(F32)).astype(BF16)
    return jnp.concatenate([high, low], axis=0)


def doubled(matrix):
    return split_rows(jnp.concatenate([matrix, matrix], axis=1))


def times(x, w):
    return lax.dot_general(x, w, (((1,), (0,)), ((), ())), preferred_element_type=F32)


def times_t(x, w):
    return lax.dot_general(x, w, (((1,), (1,)), ((), ())), preferred_element_type=F32)


def kernel(
    sources, h_near, near_blocks, basis, one, two, three, c_zero, h_zero, c_one, h_one,
    c_two, h_two, c_three, h_three, out,
    near_codes, k_zero, k_one, k_two, k_three,
    s_own, s_buf, n_buf, b_buf, t1_buf, t2_buf, t3_buf, c0_buf, c1_buf, c2_buf, c3_buf,
    bs_buf, w1_buf, p0, p1, p2, p3, own2, own3, part, o_buf,
    none, s_none, s_spare, spare0, spare1, spare2, spare3,
    load_sem, near_sem, zero_sem, code_sem, out_sem,
    send_sem, recv_sem,
):
    px, py = lax.axis_index("px"), lax.axis_index("py")
    nx, ny = lax.axis_size("px"), lax.axis_size("py")
    row3, col3 = lax.div(px, 2), lax.div(py, 2)
    blocks = tuple((i, j) for i in range(4) for j in range(4))
    inner = tuple((i, j) for i in (1, 2) for j in (1, 2))
    edge = tuple(block for block in blocks if block not in inner)

    def valid(u, v):
        ok = None
        for at, step, count in ((px, u, nx), (py, v, ny)):
            if step:
                here = at + step < count if step > 0 else at + step >= 0
                ok = here if ok is None else ok & here
        return ok

    loads = [
        pltpu.make_async_copy(sources, s_own, load_sem.at[0]),
        pltpu.make_async_copy(basis, b_buf, load_sem.at[1]),
        pltpu.make_async_copy(one, t1_buf, load_sem.at[2]),
        pltpu.make_async_copy(two, t2_buf, load_sem.at[3]),
        pltpu.make_async_copy(three, t3_buf, load_sem.at[4]),
        pltpu.make_async_copy(c_three.at[row3, col3], c3_buf, load_sem.at[5]),
        pltpu.make_async_copy(c_two, c2_buf, load_sem.at[6]),
        pltpu.make_async_copy(c_one, c1_buf, load_sem.at[7]),
        pltpu.make_async_copy(sources, s_buf.at[pl.ds(1, 4), pl.ds(1, 4)], load_sem.at[8]),
    ]
    pieces = (
        (pl.ds(0, 4), pl.ds(0, 4), pl.ds(0, 1)),
        (pl.ds(1, 2), pl.ds(1, 2), pl.ds(1, 4)),
        (pl.ds(0, 1), pl.ds(0, 4), pl.ds(1, 4)),
        (pl.ds(1, 2), pl.ds(0, 1), pl.ds(1, 4)),
        (pl.ds(1, 2), pl.ds(3, 1), pl.ds(1, 4)),
        (pl.ds(3, 1), pl.ds(0, 4), pl.ds(1, 4)),
    )
    near_loads = [
        pltpu.make_async_copy(near_blocks.at[piece], n_buf.at[piece], near_sem.at[at])
        for at, piece in enumerate(pieces)
    ]
    zero_loads = [
        pltpu.make_async_copy(c_zero.at[i], c0_buf.at[i], zero_sem) for i in range(4)
    ]
    codes = [
        pltpu.make_async_copy(h_near, near_codes, code_sem.at[0]),
        pltpu.make_async_copy(h_zero, k_zero, code_sem.at[1]),
        pltpu.make_async_copy(h_one, k_one, code_sem.at[2]),
        pltpu.make_async_copy(h_two, k_two, code_sem.at[3]),
        pltpu.make_async_copy(h_three, k_three, code_sem.at[4]),
    ]
    for load in loads[:5] + codes:
        load.start()

    barrier = pltpu.get_barrier_semaphore()
    partners = BESIDE + RING + tuple((2 * u, 2 * v) for u, v in RING)
    expected = 0
    for u, v in partners:
        ok = valid(u, v)
        expected = expected + ok.astype(jnp.int32)

        @pl.when(ok)
        def _(u=u, v=v):
            pl.semaphore_signal(barrier, inc=1, device_id=(px + u, py + v), device_id_type=MESH)

    none[...] = jnp.zeros(none.shape, BF16)
    s_none[...] = jnp.zeros(s_none.shape, BF16)

    def group_send(u, v, stride, at, src, dst, back, spare, zeros):
        ok = valid(stride * u, stride * v)

        @pl.when(ok)
        def _():
            pltpu.make_async_remote_copy(
                src_ref=src, dst_ref=dst, send_sem=send_sem.at[at], recv_sem=recv_sem.at[at],
                device_id=(px + stride * u, py + stride * v), device_id_type=MESH,
            ).start()

        @pl.when(jnp.logical_not(ok))
        def _():
            pltpu.make_async_copy(zeros, back, recv_sem.at[at]).start()
            pltpu.make_async_copy(zeros, spare, send_sem.at[at]).start()

    def halo_send(buf, n, w, at, spare, zeros, own=None):
        for u, v in BESIDE:
            if own is None:
                src = buf.at[span(u, n, w, False), span(v, n, w, False)]
            else:
                src = own.at[edge_of(u, n, w), edge_of(v, n, w)]
            there = span(-u, n, w, True), span(-v, n, w, True)
            here = span(u, n, w, True), span(v, n, w, True)
            nothing = zeros.at[pl.ds(0, here[0].size), pl.ds(0, here[1].size)]
            group_send(u, v, 1, at, src, buf.at[there], buf.at[here], spare.at[here], nothing)

    def ring_send(own, buf, stride, at, spare):
        for u, v in RING:
            here = 2 + u, 2 + v
            nothing = none.at[0, 0]
            group_send(
                u, v, stride, at, own, buf.at[2 - u, 2 - v], buf.at[here], spare.at[here], nothing
            )

    def pair_send():
        for d, (a, b) in enumerate(PAIRS):
            x = px + a * (1 - 2 * lax.rem(px, 2))
            y = py + b * (1 - 2 * lax.rem(py, 2))
            pltpu.make_async_remote_copy(
                src_ref=part.at[0], dst_ref=part.at[d + 1],
                send_sem=send_sem.at[5], recv_sem=recv_sem.at[5],
                device_id=(x, y), device_id_type=MESH,
            ).start()

    sizes = (
        s_buf.at[pl.ds(0, 5), pl.ds(0, 4)],
        p0.at[pl.ds(0, 6)],
        p0.at[pl.ds(0, 4)],
        p2.at[pl.ds(0, 4), pl.ds(0, 4)],
        p3.at[pl.ds(0, 4), pl.ds(0, 4)],
        part.at[pl.ds(1, 3)],
    )

    def arrived(at):
        pltpu.make_async_copy(sizes[at], sizes[at], recv_sem.at[at]).wait()

    def left(at):
        pltpu.make_async_copy(sizes[at], sizes[at], send_sem.at[at]).wait()

    for load in near_loads[:2]:
        load.start()
    loads[0].wait()
    loads[1].wait()
    for load in near_loads[2:4] + [loads[8], loads[5]]:
        load.start()
    totals = {}
    for i, j in blocks:
        split = split_rows(b_buf[i, j])
        bs_buf[i, j] = split
        totals[i, j] = times_t(s_own[i, j], split)
    below = {}
    for i, j in blocks:
        below[i, j] = halves(folded(totals[i, j]))
        p0[i + 2, j + 2] = below[i, j][0]
    for load in loads[2:5]:
        load.wait()
    above = {}
    for i in range(2):
        for j in range(2):
            total = jnp.zeros((32, 128), F32)
            for a in range(2):
                for b in range(2):
                    r, c = 2 * i + a, 2 * j + b
                    w = doubled(t1_buf[r, c])
                    w1_buf[r, c] = w
                    total = total + times(jnp.concatenate(below[r, c], axis=0), w)
            above[i, j] = halves(total[:16] + total[16:])
            p1[i + 2, j + 2] = above[i, j][0]
    total = jnp.zeros((32, 128), F32)
    for i in range(2):
        for j in range(2):
            total = total + times(jnp.concatenate(above[i, j], axis=0), doubled(t2_buf[i, j]))
    pair = halves(total[:16] + total[16:])
    for load in near_loads[4:] + loads[6:8]:
        load.start()
    own2[...] = pair[0]
    total = times(jnp.concatenate(pair, axis=0), doubled(t3_buf[0, 0]))
    own3[...] = halves(total[:16] + total[16:])[0]

    pl.semaphore_wait(barrier, expected)
    halo_send(s_buf, 4, 1, 0, s_spare, s_none, s_own)
    ring_send(own3, p3, 2, 4, spare3)
    ring_send(own2, p2, 1, 3, spare2)
    halo_send(p1, 2, 2, 2, spare1, none)
    halo_send(p0, 4, 2, 1, spare0, none)

    def near_product(i, j, k, buf, shift):
        code = near_codes[i, j, k]
        u = lax.shift_right_logical(code * 11, 5)
        x = buf[i + u - shift, j + code - 3 * u - shift]
        return times_t(x, n_buf[i, j, k])

    for load in codes:
        load.wait()
    near_loads[0].wait()
    near_loads[1].wait()
    for i, j in blocks:
        total = times_t(s_own[i, j], n_buf[i, j, 0])
        if (i, j) in inner:
            for k in range(1, 5):
                total = total + near_product(i, j, k, s_own, 1)
        o_buf[i, j] = total

    for load in zero_loads:
        load.start()
    loads[8].wait()
    arrived(0)
    arrived(4)

    def near_edge(some):
        for i, j in some:
            total = o_buf[i, j]
            for k in range(1, 5):
                total = total + near_product(i, j, k, s_buf, 0)
            o_buf[i, j] = total

    def coupled(matrices, codes, read, total=None):
        for k in range(0, 8, 2):
            xs, ws = [], []
            for q in (k, k + 1):
                code = codes(q)
                u = lax.shift_right_logical(code * 13, 6)
                xs.append(read(u, code - 5 * u))
                ws.append(doubled(matrices(q)))
            term = times_t(jnp.concatenate(xs, axis=1), jnp.concatenate(ws, axis=1))
            total = term if total is None else total + term
        return total

    loads[5].wait()
    for load in near_loads[2:4]:
        load.wait()
    total = coupled(
        lambda k: c3_buf[k], lambda k: k_three[row3, col3, k], lambda u, v: p3[u, v]
    )
    part[0] = halves(folded(total))[0]
    near_edge(edge[:4] + ((1, 0), (2, 0)))
    pair_send()
    for load in near_loads[4:]:
        load.wait()
    near_edge(((1, 3), (2, 3)) + edge[8:])

    for at in (3, 2, 1):
        arrived(at)
    for load in loads[6:8]:
        load.wait()
    pltpu.make_async_copy(c_zero, c0_buf, zero_sem).wait()
    field = coupled(lambda k: c2_buf[0, 0, k], lambda k: k_two[0, 0, k], lambda u, v: p2[u, v])
    ones = {}
    for i in range(2):
        for j in range(2):
            ones[i, j] = coupled(
                lambda k: c1_buf[i, j, k],
                lambda k: k_one[i, j, k],
                lambda u, v: p1[i + u, j + v],
            )
    zeros = {}
    for i, j in blocks:
        zeros[i, j] = coupled(
            lambda k: c0_buf[i, j, k],
            lambda k: k_zero[i, j, k],
            lambda u, v: p0[i + u, j + v],
        )

    arrived(5)
    w = doubled(t3_buf[0, 0])
    for d in range(4):
        field = field + times_t(part[d], w)
    x2 = halves(folded(field))[0]
    x1 = {}
    for i in range(2):
        for j in range(2):
            total = ones[i, j] + times_t(x2, doubled(t2_buf[i, j]))
            x1[i, j] = halves(folded(total))[0]
    for i, j in blocks:
        zeros[i, j] = zeros[i, j] + times_t(x1[i // 2, j // 2], w1_buf[i, j])
    outs = [pltpu.make_async_copy(o_buf.at[i], out.at[i], out_sem) for i in range(4)]
    for i, j in blocks:
        pair = halves(folded(zeros[i, j]))
        far = times(jnp.concatenate(pair, axis=0), bs_buf[i, j])
        o_buf[i, j] = o_buf[i, j] + (far[:16] + far[16:])
        if j == 3:
            outs[i].start()

    for at in range(6):
        left(at)
    pltpu.make_async_copy(o_buf, out, out_sem).wait()


def on_device(*args):
    dma = pltpu.SemaphoreType.DMA
    vmem = pltpu.VMEM
    return pl.pallas_call(
        kernel,
        out_shape=jax.ShapeDtypeStruct((4, 4, 16, 256), F32),
        in_specs=[pl.BlockSpec(memory_space=pltpu.HBM)] * len(args),
        out_specs=pl.BlockSpec(memory_space=pltpu.HBM),
        scratch_shapes=[
            pltpu.SMEM((4, 4, 5), jnp.int32),
            pltpu.SMEM((4, 4, 8), jnp.int32),
            pltpu.SMEM((2, 2, 8), jnp.int32),
            pltpu.SMEM((1, 1, 8), jnp.int32),
            pltpu.SMEM(args[14].shape, jnp.int32),
            vmem((4, 4, 16, 256), BF16),
            vmem((6, 6, 16, 256), BF16),
            vmem((4, 4, 5, 256, 256), BF16),
            vmem((4, 4, 64, 256), F32),
            vmem((4, 4, 64, 64), F32),
            vmem((2, 2, 64, 64), F32),
            vmem((1, 1, 64, 64), F32),
            vmem((4, 4, 8, 64, 64), F32),
            vmem((2, 2, 8, 64, 64), F32),
            vmem((1, 1, 8, 64, 64), F32),
            vmem((8, 64, 64), F32),
            vmem((4, 4, 128, 256), BF16),
            vmem((4, 4, 128, 128), BF16),
            vmem((8, 8, 16, 128), BF16),
            vmem((6, 6, 16, 128), BF16),
            vmem((5, 5, 16, 128), BF16),
            vmem((5, 5, 16, 128), BF16),
            vmem((16, 128), BF16),
            vmem((16, 128), BF16),
            vmem((4, 16, 128), BF16),
            vmem((4, 4, 16, 256), F32),
            vmem((4, 4, 16, 128), BF16),
            vmem((4, 4, 16, 256), BF16),
            vmem((6, 6, 16, 256), BF16),
            vmem((8, 8, 16, 128), BF16),
            vmem((6, 6, 16, 128), BF16),
            vmem((5, 5, 16, 128), BF16),
            vmem((5, 5, 16, 128), BF16),
            dma((9,)),
            dma((6,)),
            dma,
            dma((5,)),
            dma,
            dma((6,)),
            dma((6,)),
        ],
        compiler_params=pltpu.CompilerParams(
            collective_id=0, has_side_effects=True, vmem_limit_bytes=60 * 1024 * 1024
        ),
        name="patches",
    )(*args)


def solution(mesh):
    grid = P("px", "py")
    placed = (grid,) * 13 + (P(), P())
    return jax.shard_map(
        on_device, mesh=mesh, in_specs=placed, out_specs=grid, check_vma=False
    )
```

```python
import jax
import jax.numpy as jnp
from jax import lax
from jax.experimental import pallas as pl
from jax.experimental.pallas import tpu as pltpu
from jax.sharding import PartitionSpec as P

BF16 = jnp.bfloat16
F32 = jnp.float32
MESH = pl.DeviceIdType.MESH

BESIDE = tuple((u, v) for u in (-1, 0, 1) for v in (-1, 0, 1) if (u, v) != (0, 0))
RING = tuple((u, v) for u in range(-2, 3) for v in range(-2, 3) if max(abs(u), abs(v)) == 2)
PAIRS = ((0, 1), (1, 0), (1, 1))


def span(step, count, width, halo):
    if step == 0:
        return pl.ds(width, count)
    if halo:
        return pl.ds(0, width) if step < 0 else pl.ds(width + count, width)
    return pl.ds(width, width) if step < 0 else pl.ds(count, width)


def edge_of(step, count, width):
    if step == 0:
        return pl.ds(0, count)
    return pl.ds(0, width) if step < 0 else pl.ds(count - width, width)


def folded(total):
    return total + pltpu.roll(total, 64, 1)


def halves(value):
    lane = lax.broadcasted_iota(jnp.int32, value.shape, 1)
    high = value.astype(BF16).astype(F32)
    low = value - high
    first = lane < 64
    return jnp.where(first, high, low).astype(BF16), jnp.where(first, low, high).astype(BF16)


def split_rows(matrix):
    high = matrix.astype(BF16)
    low = (matrix - high.astype(F32)).astype(BF16)
    return jnp.concatenate([high, low], axis=0)


def doubled(matrix):
    return split_rows(jnp.concatenate([matrix, matrix], axis=1))


def times(x, w):
    return lax.dot_general(x, w, (((1,), (0,)), ((), ())), preferred_element_type=F32)


def times_t(x, w):
    return lax.dot_general(x, w, (((1,), (1,)), ((), ())), preferred_element_type=F32)


def kernel(
    sources, h_near, near_blocks, basis, one, two, three, c_zero, h_zero, c_one, h_one,
    c_two, h_two, c_three, h_three, out,
    near_codes, k_zero, k_one, k_two, k_three,
    s_own, s_buf, n_buf, b_buf, t1_buf, t2_buf, t3_buf, c0_buf, c1_buf, c2_buf, c3_buf,
    bs_buf, w1_buf, p0, p1, p2, p3, own2, own3, part, o_buf,
    none, s_none, s_spare, spare0, spare1, spare2, spare3,
    load_sem, near_sem, zero_sem, code_sem, out_sem,
    send_sem, recv_sem,
):
    px, py = lax.axis_index("px"), lax.axis_index("py")
    nx, ny = lax.axis_size("px"), lax.axis_size("py")
    row3, col3 = lax.div(px, 2), lax.div(py, 2)
    blocks = tuple((i, j) for i in range(4) for j in range(4))
    inner = tuple((i, j) for i in (1, 2) for j in (1, 2))
    edge = tuple(block for block in blocks if block not in inner)

    def valid(u, v):
        ok = None
        for at, step, count in ((px, u, nx), (py, v, ny)):
            if step:
                here = at + step < count if step > 0 else at + step >= 0
                ok = here if ok is None else ok & here
        return ok

    loads = [
        pltpu.make_async_copy(sources, s_own, load_sem.at[0]),
        pltpu.make_async_copy(basis, b_buf, load_sem.at[1]),
        pltpu.make_async_copy(one, t1_buf, load_sem.at[2]),
        pltpu.make_async_copy(two, t2_buf, load_sem.at[3]),
        pltpu.make_async_copy(three, t3_buf, load_sem.at[4]),
        pltpu.make_async_copy(c_three.at[row3, col3], c3_buf, load_sem.at[5]),
        pltpu.make_async_copy(c_two, c2_buf, load_sem.at[6]),
        pltpu.make_async_copy(c_one, c1_buf, load_sem.at[7]),
        pltpu.make_async_copy(sources, s_buf.at[pl.ds(1, 4), pl.ds(1, 4)], load_sem.at[8]),
    ]
    pieces = (
        (pl.ds(0, 4), pl.ds(0, 4), pl.ds(0, 1)),
        (pl.ds(1, 2), pl.ds(1, 2), pl.ds(1, 4)),
        (pl.ds(0, 1), pl.ds(0, 4), pl.ds(1, 4)),
        (pl.ds(1, 2), pl.ds(0, 1), pl.ds(1, 4)),
        (pl.ds(1, 2), pl.ds(3, 1), pl.ds(1, 4)),
        (pl.ds(3, 1), pl.ds(0, 4), pl.ds(1, 4)),
    )
    near_loads = [
        pltpu.make_async_copy(near_blocks.at[piece], n_buf.at[piece], near_sem.at[at])
        for at, piece in enumerate(pieces)
    ]
    zero_loads = [
        pltpu.make_async_copy(c_zero.at[i], c0_buf.at[i], zero_sem) for i in range(4)
    ]
    codes = [
        pltpu.make_async_copy(h_near, near_codes, code_sem.at[0]),
        pltpu.make_async_copy(h_zero, k_zero, code_sem.at[1]),
        pltpu.make_async_copy(h_one, k_one, code_sem.at[2]),
        pltpu.make_async_copy(h_two, k_two, code_sem.at[3]),
        pltpu.make_async_copy(h_three, k_three, code_sem.at[4]),
    ]
    for load in loads[:5] + codes:
        load.start()

    barrier = pltpu.get_barrier_semaphore()
    partners = BESIDE + RING + tuple((2 * u, 2 * v) for u, v in RING)
    expected = 0
    for u, v in partners:
        ok = valid(u, v)
        expected = expected + ok.astype(jnp.int32)

        @pl.when(ok)
        def _(u=u, v=v):
            pl.semaphore_signal(barrier, inc=1, device_id=(px + u, py + v), device_id_type=MESH)

    none[...] = jnp.zeros(none.shape, BF16)
    s_none[...] = jnp.zeros(s_none.shape, BF16)

    def group_send(u, v, stride, at, src, dst, back, spare, zeros):
        ok = valid(stride * u, stride * v)

        @pl.when(ok)
        def _():
            pltpu.make_async_remote_copy(
                src_ref=src, dst_ref=dst, send_sem=send_sem.at[at], recv_sem=recv_sem.at[at],
                device_id=(px + stride * u, py + stride * v), device_id_type=MESH,
            ).start()

        @pl.when(jnp.logical_not(ok))
        def _():
            pltpu.make_async_copy(zeros, back, recv_sem.at[at]).start()
            pltpu.make_async_copy(zeros, spare, send_sem.at[at]).start()

    def halo_send(buf, n, w, at, spare, zeros, own=None):
        for u, v in BESIDE:
            if own is None:
                src = buf.at[span(u, n, w, False), span(v, n, w, False)]
            else:
                src = own.at[edge_of(u, n, w), edge_of(v, n, w)]
            there = span(-u, n, w, True), span(-v, n, w, True)
            here = span(u, n, w, True), span(v, n, w, True)
            nothing = zeros.at[pl.ds(0, here[0].size), pl.ds(0, here[1].size)]
            group_send(u, v, 1, at, src, buf.at[there], buf.at[here], spare.at[here], nothing)

    def ring_send(own, buf, stride, at, spare):
        for u, v in RING:
            here = 2 + u, 2 + v
            nothing = none.at[0, 0]
            group_send(
                u, v, stride, at, own, buf.at[2 - u, 2 - v], buf.at[here], spare.at[here], nothing
            )

    def pair_send():
        for d, (a, b) in enumerate(PAIRS):
            x = px + a * (1 - 2 * lax.rem(px, 2))
            y = py + b * (1 - 2 * lax.rem(py, 2))
            pltpu.make_async_remote_copy(
                src_ref=part.at[0], dst_ref=part.at[d + 1],
                send_sem=send_sem.at[5], recv_sem=recv_sem.at[5],
                device_id=(x, y), device_id_type=MESH,
            ).start()

    sizes = (
        s_buf.at[pl.ds(0, 5), pl.ds(0, 4)],
        p0.at[pl.ds(0, 6)],
        p0.at[pl.ds(0, 4)],
        p2.at[pl.ds(0, 4), pl.ds(0, 4)],
        p3.at[pl.ds(0, 4), pl.ds(0, 4)],
        part.at[pl.ds(1, 3)],
    )

    def arrived(at):
        pltpu.make_async_copy(sizes[at], sizes[at], recv_sem.at[at]).wait()

    def left(at):
        pltpu.make_async_copy(sizes[at], sizes[at], send_sem.at[at]).wait()

    for load in near_loads[:2]:
        load.start()
    loads[0].wait()
    loads[1].wait()
    for load in near_loads[2:4] + [loads[8], loads[5]]:
        load.start()
    totals = {}
    for i, j in blocks:
        split = split_rows(b_buf[i, j])
        bs_buf[i, j] = split
        totals[i, j] = times_t(s_own[i, j], split)
    below = {}
    for i, j in blocks:
        below[i, j] = halves(folded(totals[i, j]))
        p0[i + 2, j + 2] = below[i, j][0]
    for load in loads[2:5]:
        load.wait()
    above = {}
    for i in range(2):
        for j in range(2):
            total = jnp.zeros((32, 128), F32)
            for a in range(2):
                for b in range(2):
                    r, c = 2 * i + a, 2 * j + b
                    w = doubled(t1_buf[r, c])
                    w1_buf[r, c] = w
                    total = total + times(jnp.concatenate(below[r, c], axis=0), w)
            above[i, j] = halves(total[:16] + total[16:])
            p1[i + 2, j + 2] = above[i, j][0]
    total = jnp.zeros((32, 128), F32)
    for i in range(2):
        for j in range(2):
            total = total + times(jnp.concatenate(above[i, j], axis=0), doubled(t2_buf[i, j]))
    pair = halves(total[:16] + total[16:])
    for load in near_loads[4:] + loads[6:8]:
        load.start()
    own2[...] = pair[0]
    total = times(jnp.concatenate(pair, axis=0), doubled(t3_buf[0, 0]))
    own3[...] = halves(total[:16] + total[16:])[0]

    pl.semaphore_wait(barrier, expected)
    halo_send(s_buf, 4, 1, 0, s_spare, s_none, s_own)
    ring_send(own3, p3, 2, 4, spare3)
    ring_send(own2, p2, 1, 3, spare2)
    halo_send(p1, 2, 2, 2, spare1, none)
    halo_send(p0, 4, 2, 1, spare0, none)

    def near_product(i, j, k, buf, shift):
        code = near_codes[i, j, k]
        u = lax.shift_right_logical(code * 11, 5)
        x = buf[i + u - shift, j + code - 3 * u - shift]
        return times_t(x, n_buf[i, j, k])

    for load in codes:
        load.wait()
    near_loads[0].wait()
    near_loads[1].wait()
    for i, j in blocks:
        total = times_t(s_own[i, j], n_buf[i, j, 0])
        if (i, j) in inner:
            for k in range(1, 5):
                total = total + near_product(i, j, k, s_own, 1)
        o_buf[i, j] = total

    for load in zero_loads:
        load.start()
    loads[8].wait()
    arrived(0)

    def near_edge(some):
        for i, j in some:
            total = o_buf[i, j]
            for k in range(1, 5):
                total = total + near_product(i, j, k, s_buf, 0)
            o_buf[i, j] = total

    def coupled(matrices, codes, read, total=None):
        for k in range(0, 8, 2):
            xs, ws = [], []
            for q in (k, k + 1):
                code = codes(q)
                u = lax.shift_right_logical(code * 13, 6)
                xs.append(read(u, code - 5 * u))
                ws.append(doubled(matrices(q)))
            term = times_t(jnp.concatenate(xs, axis=1), jnp.concatenate(ws, axis=1))
            total = term if total is None else total + term
        return total

    for load in near_loads[2:4]:
        load.wait()
    near_edge(edge[:4] + ((1, 0), (2, 0)))

    loads[5].wait()
    arrived(4)
    total = coupled(
        lambda k: c3_buf[k], lambda k: k_three[row3, col3, k], lambda u, v: p3[u, v]
    )
    part[0] = halves(folded(total))[0]
    pair_send()
    for load in near_loads[4:]:
        load.wait()
    near_edge(((1, 3), (2, 3)) + edge[8:])

    for at in (3, 2, 1):
        arrived(at)
    for load in loads[6:8]:
        load.wait()
    pltpu.make_async_copy(c_zero, c0_buf, zero_sem).wait()
    field = coupled(lambda k: c2_buf[0, 0, k], lambda k: k_two[0, 0, k], lambda u, v: p2[u, v])
    ones = {}
    for i in range(2):
        for j in range(2):
            ones[i, j] = coupled(
                lambda k: c1_buf[i, j, k],
                lambda k: k_one[i, j, k],
                lambda u, v: p1[i + u, j + v],
            )
    zeros = {}
    for i, j in blocks:
        zeros[i, j] = coupled(
            lambda k: c0_buf[i, j, k],
            lambda k: k_zero[i, j, k],
            lambda u, v: p0[i + u, j + v],
        )

    arrived(5)
    w = doubled(t3_buf[0, 0])
    for d in range(4):
        field = field + times_t(part[d], w)
    x2 = halves(folded(field))[0]
    x1 = {}
    for i in range(2):
        for j in range(2):
            total = ones[i, j] + times_t(x2, doubled(t2_buf[i, j]))
            x1[i, j] = halves(folded(total))[0]
    for i, j in blocks:
        zeros[i, j] = zeros[i, j] + times_t(x1[i // 2, j // 2], w1_buf[i, j])
    outs = [pltpu.make_async_copy(o_buf.at[i], out.at[i], out_sem) for i in range(4)]
    for i, j in blocks:
        pair = halves(folded(zeros[i, j]))
        far = times(jnp.concatenate(pair, axis=0), bs_buf[i, j])
        o_buf[i, j] = o_buf[i, j] + (far[:16] + far[16:])
        if j == 3:
            outs[i].start()

    for at in range(6):
        left(at)
    pltpu.make_async_copy(o_buf, out, out_sem).wait()


def on_device(*args):
    dma = pltpu.SemaphoreType.DMA
    vmem = pltpu.VMEM
    return pl.pallas_call(
        kernel,
        out_shape=jax.ShapeDtypeStruct((4, 4, 16, 256), F32),
        in_specs=[pl.BlockSpec(memory_space=pltpu.HBM)] * len(args),
        out_specs=pl.BlockSpec(memory_space=pltpu.HBM),
        scratch_shapes=[
            pltpu.SMEM((4, 4, 5), jnp.int32),
            pltpu.SMEM((4, 4, 8), jnp.int32),
            pltpu.SMEM((2, 2, 8), jnp.int32),
            pltpu.SMEM((1, 1, 8), jnp.int32),
            pltpu.SMEM(args[14].shape, jnp.int32),
            vmem((4, 4, 16, 256), BF16),
            vmem((6, 6, 16, 256), BF16),
            vmem((4, 4, 5, 256, 256), BF16),
            vmem((4, 4, 64, 256), F32),
            vmem((4, 4, 64, 64), F32),
            vmem((2, 2, 64, 64), F32),
            vmem((1, 1, 64, 64), F32),
            vmem((4, 4, 8, 64, 64), F32),
            vmem((2, 2, 8, 64, 64), F32),
            vmem((1, 1, 8, 64, 64), F32),
            vmem((8, 64, 64), F32),
            vmem((4, 4, 128, 256), BF16),
            vmem((4, 4, 128, 128), BF16),
            vmem((8, 8, 16, 128), BF16),
            vmem((6, 6, 16, 128), BF16),
            vmem((5, 5, 16, 128), BF16),
            vmem((5, 5, 16, 128), BF16),
            vmem((16, 128), BF16),
            vmem((16, 128), BF16),
            vmem((4, 16, 128), BF16),
            vmem((4, 4, 16, 256), F32),
            vmem((4, 4, 16, 128), BF16),
            vmem((4, 4, 16, 256), BF16),
            vmem((6, 6, 16, 256), BF16),
            vmem((8, 8, 16, 128), BF16),
            vmem((6, 6, 16, 128), BF16),
            vmem((5, 5, 16, 128), BF16),
            vmem((5, 5, 16, 128), BF16),
            dma((9,)),
            dma((6,)),
            dma,
            dma((5,)),
            dma,
            dma((6,)),
            dma((6,)),
        ],
        compiler_params=pltpu.CompilerParams(
            collective_id=0, has_side_effects=True, vmem_limit_bytes=60 * 1024 * 1024
        ),
        name="patches",
    )(*args)


def solution(mesh):
    grid = P("px", "py")
    placed = (grid,) * 13 + (P(), P())
    return jax.shard_map(
        on_device, mesh=mesh, in_specs=placed, out_specs=grid, check_vma=False
    )
```
